32 devices in a mesh: groups: 2 (over x), tm: 16 (over z, y, core).
Axes of the slice: x: 2, y: 2, z: 4, core: 2. Of those that a mesh axis runs over, the one named last changes fastest.
Arguments:
- obs_weights: bfloat16 [64, 512, 128], P('groups', 'tm'), parts along dimension 0, may hold values from -0.375 to 0.375
- obs_values: float32 [64, 512], P('groups', 'tm'), parts along dimension 0, may hold values from -6 to 6
- obs_precision: float32 [64, 512], P('groups', 'tm'), parts along dimension 0, may hold values from 0.3 to 3
- obs_block: int32 [64, 512], P('groups', 'tm'), parts along dimension 0, may hold values from 0 to 1
- obs_count: int32 [64, 16], P('groups', 'tm'), parts along dimension 0, may hold values from 8 to 32, as said below
- prior_precision_entries: float32 [256], replicated, may hold values from 1 to 512
- transition: float32 [256, 256], replicated, may hold values from -1.01 to 1.01
- initial_state: float32 [512], P('groups'), parts along dimension 0, may hold values from -6 to 6
Outputs:
- filtered: float32 [64, 256], P(('groups', 'tm')), parts along dimension 0
- smoothed: float32 [64, 256], P(('groups', 'tm')), parts along dimension 0
The draws below stay inside these ranges and needn't reach their ends.
There are 2 independent parts, one for each index of `groups`. The reference program is written for one: setup_inputs(seed, part) draws one part's arguments, and reference() takes and returns one part's arrays. A program takes and returns all parts, laid end to end along the dimension named above; an argument that names none is the same for every part. Nothing has to cross between parts.
Inputs may be any that keep to these rules, and one draw needn't show every extreme that they name: `obs_count`: no index of tm has more than 32 live rows at a step, and at every step some index has exactly 32.
All inputs are finite; a program needn't handle non-finite values.
Results may differ from the reference program's by a relative error of at most 0.0003.
Values sent between devices are 32-bit elements; how exact they have to be, the bound alone decides.
A program may use at most 64 MiB of HBM per device.

```python
import math
import jax
import jax.numpy as jnp
from jax import lax

NS = 256
BLK = 128
ROWS = 32
TSTEPS = 32
OBS = 512
NB = 2
N_TM = 16


def draw_obs_count(key, part):
    first_key, second_key = jax.random.split(key)
    base = jax.random.randint(first_key, (TSTEPS, N_TM), max(1, ROWS // 4), ROWS + 1)
    chosen = jax.random.randint(second_key, (TSTEPS, 1), 0, N_TM)
    marked = jnp.arange(N_TM, dtype=jnp.int32)[None, :] == chosen
    return jnp.where(marked, ROWS, base).astype(jnp.int32)


def draw_transition(key, part):
    rate_key, angle_key, couple_key = jax.random.split(key, 3)
    half = NS // 2
    rates = jnp.exp(-jax.random.uniform(rate_key, (NS,), jnp.float32, 0.0, 0.5) / TSTEPS)
    angles = jax.random.uniform(angle_key, (half,), jnp.float32, -1.0, 1.0)
    cosines = jnp.concatenate([jnp.cos(angles), jnp.cos(angles)])
    sines = jnp.sin(angles)
    naught = jnp.zeros((half,), jnp.float32)
    upper_band = jnp.eye(NS, k=half, dtype=jnp.float32) * jnp.concatenate([-sines, naught])[:, None]
    lower_band = jnp.eye(NS, k=-half, dtype=jnp.float32) * jnp.concatenate([naught, sines])[:, None]
    rotation = jnp.eye(NS, dtype=jnp.float32) * cosines[:, None] + upper_band + lower_band
    spread = 0.5 / (TSTEPS * math.sqrt(NS))
    coupling = jnp.clip(jax.random.normal(couple_key, (NS, NS), jnp.float32) * spread, -3.0 * spread, 3.0 * spread)
    return (rates[:, None] * rotation + coupling).astype(jnp.float32)


def touch_ends(values, rng, low, largest):
    spot = [jax.random.randint(jax.random.fold_in(rng, axis), (), 0, length) for axis, length in enumerate(values.shape)]
    longest = values.shape.index(max(values.shape))
    beside = spot[:longest] + [(spot[longest] + 1) % values.shape[longest]] + spot[longest + 1:]
    return values.at[tuple(spot)].set(low).at[tuple(beside)].set(largest)


def block_levels(stream_key, shape, cuts, smallest, high):
    loudness = 1.0
    for position, shards_of in cuts:
        draws = jax.random.uniform(jax.random.fold_in(jax.random.fold_in(stream_key, 6), position), (shards_of,), jnp.float32, smallest / len(cuts), high / len(cuts))
        loudness = loudness * jnp.repeat(jnp.exp(draws), shape[position] // shards_of).reshape((-1,) + (1,) * (len(shape) - 1 - position))
    return loudness


def scatter_about(rng, shape, deviation, limit, cuts=(), kind=jnp.bfloat16):
    level = block_levels(rng, shape, cuts, -0.22, 0.18) if cuts else 1.0
    drawn = jax.random.normal(rng, shape, jnp.float32) * deviation * level
    return jnp.minimum(jnp.maximum(drawn, -limit), limit).astype(kind)


def setup_inputs(seed: int = 0, part: int = 0) -> dict:
    seeds = jax.random.split(jax.random.key(seed), 9)
    part_splits = jax.random.split(jax.random.fold_in(seeds[8], part), 9)
    obs_weights = scatter_about(part_splits[0], (TSTEPS, OBS, BLK), (OBS // NB) ** -0.5, 0.375, ((1, 16),))
    obs_values = scatter_about(part_splits[1], (TSTEPS, OBS), 1.0, 6.0, ((1, 16),), jnp.float32)
    obs_precision = jnp.clip(jnp.exp(math.log(3.0) - 2.3025851 * jax.random.uniform(part_splits[2], (TSTEPS, OBS), jnp.float32) ** block_levels(part_splits[2], (TSTEPS, OBS), ((1, 16),), -0.2, 0.2)), 0.3, 3.0)
    obs_block = touch_ends(jax.random.randint(part_splits[3], (TSTEPS, OBS), 0, NB), jax.random.fold_in(part_splits[3], 1), 0, NB - 1).astype(jnp.int32)
    obs_count = draw_obs_count(jax.random.fold_in(jax.random.fold_in(seeds[8], part), 71), part)
    prior_precision_entries = jnp.clip(jnp.exp(jax.random.uniform(seeds[5], (NS,), jnp.float32, math.log(1.0), math.log(512.0))), 1.0, 512.0)
    transition = draw_transition(jax.random.fold_in(seeds[8], 71), part)
    initial_state = scatter_about(part_splits[7], (NS,), 1.0, 6.0, (), jnp.float32)
    return dict(obs_weights=obs_weights, obs_values=obs_values, obs_precision=obs_precision, obs_block=obs_block, obs_count=obs_count, prior_precision_entries=prior_precision_entries, transition=transition, initial_state=initial_state)


def information_terms(obs_weights, obs_values, obs_precision, obs_block, allowed, row_count, block_count):
    weights = obs_weights.astype(jnp.float32)
    steps_here = obs_weights.shape[0]
    local_row = jnp.arange(obs_values.shape[1], dtype=jnp.int32) % row_count
    valid = (local_row[None, :] < allowed).astype(jnp.float32)
    weighted = valid * obs_precision
    selector = (obs_block[:, :, None] == jnp.arange(block_count, dtype=jnp.int32)[None, None, :]).astype(jnp.float32)
    information = jnp.einsum("trb,trc->tbc", selector * (weighted * obs_values)[:, :, None], weights, precision=lax.Precision.HIGHEST).reshape(steps_here, -1)
    precision_sum = jnp.einsum("trb,trc->tbc", selector * weighted[:, :, None], weights * weights, precision=lax.Precision.HIGHEST).reshape(steps_here, -1)
    return information, precision_sum


def filter_steps(start_state, information, precision_sum, background, transition):
    def advance(state, inputs):
        info_row, prec_row = inputs
        ahead = jnp.dot(transition, state, precision=lax.Precision.HIGHEST)
        state = (background * ahead + info_row) / (background + prec_row)
        return state, state
    final, state_sequence = lax.scan(advance, start_state, (information, precision_sum))
    return state_sequence


def smooth_steps(after_state, filtered, smooth_gain, transition):
    def retreat(next_state, inputs):
        present_state, gain_row = inputs
        predicted_state = jnp.dot(transition, present_state, precision=lax.Precision.HIGHEST)
        state_increment = jnp.dot(next_state - predicted_state, transition, precision=lax.Precision.HIGHEST)
        state = present_state + gain_row * state_increment
        return state, state
    final, state_sequence = lax.scan(retreat, after_state, (filtered, smooth_gain), reverse=True)
    return state_sequence


def reference(obs_weights, obs_values, obs_precision, obs_block, obs_count, prior_precision_entries, transition, initial_state):
    allowed = jnp.repeat(obs_count, ROWS, axis=1)
    block_count = NS // BLK

    def per_step(items):
        weight_row, value_row, prec_row, block_row_slice, count_row = items
        information, precision_sum = information_terms(weight_row[None], value_row[None], prec_row[None], block_row_slice[None], count_row[None], ROWS, block_count)
        return information[0], precision_sum[0]

    information, precision_sum = lax.map(per_step, (obs_weights, obs_values, obs_precision, obs_block, allowed))
    filtered = filter_steps(initial_state, information, precision_sum, prior_precision_entries, transition)
    smooth_gain = prior_precision_entries[None, :] / (prior_precision_entries[None, :] + precision_sum)
    final_step = (jnp.arange(TSTEPS, dtype=jnp.int32) == TSTEPS - 1)[:, None]
    smooth_gain = jnp.where(final_step, jnp.zeros_like(smooth_gain), smooth_gain)
    smoothed = smooth_steps(jnp.zeros_like(initial_state), filtered, smooth_gain, transition)
    return (filtered, smoothed)
```

```python
import functools

import jax
import jax.numpy as jnp
from jax import lax
from jax.experimental import pallas as pl
from jax.experimental.pallas import tpu as pltpu
from jax.sharding import PartitionSpec as P

MESH = pl.DeviceIdType.MESH
LANES = 128


def two_parts(x):
    high = x.astype(jnp.bfloat16)
    low = (x - high.astype(jnp.float32)).astype(jnp.bfloat16)
    return high, low


def observe_kernel(
    n, weights_ref, values_ref, precision_ref, block_ref, count_ref, out_ref,
    part, inbox, scatter_send, scatter_recv, gather_send, gather_recv,
):
    me = lax.axis_index("tm")
    steps, rows, width = weights_ref.shape
    barrier = pltpu.get_barrier_semaphore()
    for k in range(1, n):
        pl.semaphore_signal(
            barrier, inc=1, device_id={"tm": lax.rem(me + k, n)}, device_id_type=MESH
        )

    group = 8
    depth = group * rows
    lane = lax.broadcasted_iota(jnp.int32, (group, depth), 1)
    line = lax.broadcasted_iota(jnp.int32, (group, depth), 0)
    diagonal = lane // rows == line
    row = lax.broadcasted_iota(jnp.int32, (group, rows), 1)
    for chunk in range(steps // group):
        here = pl.ds(chunk * group, group)
        weighted = jnp.where(row < count_ref[here, :], precision_ref[here, :], 0.0)
        moment = weighted * values_ref[here, :]
        which = block_ref[here, :]

        def left(coefficient):
            lines = []
            for b in range(2):
                chosen = jnp.where(which == b, coefficient, 0.0)
                wide = jnp.concatenate([chosen] * group, axis=1)
                lines.append(jnp.where(diagonal, wide, 0.0))
            high, low = two_parts(jnp.concatenate(lines, axis=0))
            return jnp.concatenate([high, low], axis=0)

        w = weights_ref[here].reshape(depth, width)
        wf = w.astype(jnp.float32)
        square_high, square_low = two_parts(wf * wf)
        dot = functools.partial(jnp.dot, preferred_element_type=jnp.float32)
        info = dot(left(moment), w)
        info = info[: 2 * group] + info[2 * group :]
        lp = left(weighted)
        prec = dot(lp, square_high)
        prec = prec[: 2 * group] + prec[2 * group :] + dot(lp[: 2 * group], square_low)
        for kind, block in ((0, info), (1, prec)):
            for b in range(2):
                for j in range(group // 2):
                    part[chunk * (group // 2) + j, kind * 4 + b * 2 : kind * 4 + b * 2 + 2, :] = block[
                        b * group + 2 * j : b * group + 2 * j + 2
                    ]

    pl.semaphore_wait(barrier, n - 1)
    scatters = []
    for k in range(1, n):
        peer = lax.rem(me + k, n)
        copy = pltpu.make_async_remote_copy(
            src_ref=part.at[peer], dst_ref=inbox.at[k], send_sem=scatter_send.at[k],
            recv_sem=scatter_recv.at[k], device_id={"tm": peer}, device_id_type=MESH,
        )
        copy.start()
        scatters.append(copy)
    total = part[me]
    for k in range(1, n):
        scatters[k - 1].wait_recv()
        total = total + inbox[k]
    out_ref[me] = total
    gathers = []
    for k in range(1, n):
        peer = lax.rem(me + k, n)
        copy = pltpu.make_async_remote_copy(
            src_ref=out_ref.at[me], dst_ref=out_ref.at[me], send_sem=gather_send.at[k],
            recv_sem=gather_recv.at[k], device_id={"tm": peer}, device_id_type=MESH,
        )
        copy.start()
        gathers.append(copy)
    for copy in scatters:
        copy.wait_send()
    for copy in gathers:
        copy.wait()


def chain_kernel(
    n, sums_ref, background_ref, transition_ref, start_ref, filtered_ref, smoothed_ref,
    turned, gain_row, add_row, gain_col, add_col, ahead_row, ahead_col, state_row, state_col,
    smooth_row, smooth_col,
):
    me = lax.axis_index("tm")
    size = transition_ref.shape[0]
    groups = size // 8

    for i in range(2):
        for j in range(2):
            turned[j * LANES : (j + 1) * LANES, i * LANES : (i + 1) * LANES] = transition_ref[
                i * LANES : (i + 1) * LANES, j * LANES : (j + 1) * LANES
            ].T

    for b in range(2):
        background = background_ref[:, b * LANES : (b + 1) * LANES]
        for parity in range(2):
            info = sums_ref[:, b * 2 + parity, :]
            denominator = background + sums_ref[:, 4 + b * 2 + parity, :]
            gain = background / denominator
            add = info / denominator
            if parity == 1:
                gain_row[:, 0, b * LANES : (b + 1) * LANES] = gain
                add_row[:, 0, b * LANES : (b + 1) * LANES] = add
            else:
                gain_t, add_t = gain.T, add.T
                for d in range(n):
                    at = pl.ds(b * LANES, LANES)
                    gain_col[d, at, :] = jnp.broadcast_to(gain_t[:, d : d + 1], (LANES, LANES))
                    add_col[d, at, :] = jnp.broadcast_to(add_t[:, d : d + 1], (LANES, LANES))

    def to_col(matrix, x, finish):
        left = jnp.broadcast_to(x[:, :LANES], (8, LANES))
        right = jnp.broadcast_to(x[:, LANES:], (8, LANES))
        for g in range(groups):
            at = pl.ds(8 * g, 8)
            p = matrix[at, :LANES] * left + matrix[at, LANES:] * right
            finish(at, jnp.broadcast_to(jnp.sum(p, axis=1, keepdims=True), (8, LANES)))

    def to_row(matrix, x_of):
        lines = 4
        totals = [[None, None] for _ in range(lines)]
        for g in range(groups):
            at = pl.ds(8 * g, 8)
            x = x_of(at)
            for h in range(2):
                p = matrix[at, h * LANES : (h + 1) * LANES] * x
                held = totals[g % lines][h]
                totals[g % lines][h] = p if held is None else held + p
        out = []
        for h in range(2):
            s = (totals[0][h] + totals[1][h]) + (totals[2][h] + totals[3][h])
            out.append(jnp.sum(s, axis=0, keepdims=True))
        return jnp.concatenate(out, axis=1)

    def forward(d, x):
        def finish(at, z):
            ahead_col[d, at, :] = z
            state_col[d, at, :] = gain_col[d, at, :] * z + add_col[d, at, :]

        to_col(transition_ref, x, finish)
        z = to_row(turned, lambda at: state_col[d, at, :])
        x = gain_row[d] * z + add_row[d]
        ahead_row[d] = z
        state_row[d] = x
        return x

    last = lax.fori_loop(0, n, forward, start_ref[...])

    def to_even(d, s):
        def finish(at, y):
            smooth_col[d, at, :] = state_col[d, at, :] + gain_col[d, at, :] * y

        to_col(turned, s - ahead_row[d], finish)

    def backward(i, s):
        d = n - 1 - i
        to_even(d, s)
        y = to_row(transition_ref, lambda at: smooth_col[d, at, :] - ahead_col[d, at, :])
        s = state_row[d - 1] + gain_row[d - 1] * y
        smooth_row[d - 1] = s
        return s

    smooth_row[n - 1] = last
    first = lax.fori_loop(0, n - 1, backward, last)
    to_even(0, first)

    diagonal = lax.broadcasted_iota(jnp.int32, (LANES, LANES), 0) == lax.broadcasted_iota(
        jnp.int32, (LANES, LANES), 1
    )
    for col, line, out in ((state_col, state_row, filtered_ref), (smooth_col, smooth_row, smoothed_ref)):
        for b in range(2):
            block = col[me, b * LANES : (b + 1) * LANES, :]
            out[0:1, b * LANES : (b + 1) * LANES] = jnp.sum(
                jnp.where(diagonal, block, 0.0), axis=0, keepdims=True
            )
        out[1:2, :] = line[me]


def shards(
    obs_weights, obs_values, obs_precision, obs_block, obs_count,
    prior_precision_entries, transition, initial_state,
):
    n = lax.axis_size("tm")
    size = transition.shape[0]
    vmem = pl.BlockSpec(memory_space=pltpu.VMEM)
    sums = pl.pallas_call(
        functools.partial(observe_kernel, n),
        out_shape=jax.ShapeDtypeStruct((n, 8, LANES), jnp.float32),
        in_specs=[vmem] * 5,
        out_specs=vmem,
        scratch_shapes=[
            pltpu.VMEM((n, 8, LANES), jnp.float32),
            pltpu.VMEM((n, 8, LANES), jnp.float32),
            pltpu.SemaphoreType.DMA((n,)),
            pltpu.SemaphoreType.DMA((n,)),
            pltpu.SemaphoreType.DMA((n,)),
            pltpu.SemaphoreType.DMA((n,)),
        ],
        compiler_params=pltpu.CompilerParams(collective_id=0, has_side_effects=True),
        name="observe",
    )(obs_weights, obs_values, obs_precision, obs_block, obs_count)
    row = pltpu.VMEM((n, 1, size), jnp.float32)
    col = pltpu.VMEM((n, size, LANES), jnp.float32)
    out = jax.ShapeDtypeStruct((2, size), jnp.float32)
    return pl.pallas_call(
        functools.partial(chain_kernel, n),
        out_shape=(out, out),
        in_specs=[vmem] * 4,
        out_specs=(vmem, vmem),
        scratch_shapes=[
            pltpu.VMEM((size, size), jnp.float32),
            row, row, col, col, row, col, row, col, row, col,
        ],
        compiler_params=pltpu.CompilerParams(vmem_limit_bytes=56 * 1024 * 1024),
        name="chain",
    )(sums, prior_precision_entries[None], transition, initial_state[None])


def solution(mesh):
    placed = (
        P("groups", "tm", None),
        P("groups", "tm"),
        P("groups", "tm"),
        P("groups", "tm"),
        P("groups", "tm"),
        P(),
        P(),
        P("groups"),
    )
    return jax.shard_map(
        shards,
        mesh=mesh,
        in_specs=placed,
        out_specs=(P(("groups", "tm"), None), P(("groups", "tm"), None)),
        check_vma=False,
    )
```

```python
import functools

import jax
import jax.numpy as jnp
from jax import lax
from jax.experimental import pallas as pl
from jax.experimental.pallas import tpu as pltpu
from jax.sharding import PartitionSpec as P

MESH = pl.DeviceIdType.MESH
LANES = 128


def two_parts(x):
    high = x.astype(jnp.bfloat16)
    low = (x - high.astype(jnp.float32)).astype(jnp.bfloat16)
    return high, low


def kernel(
    n, weights_hbm, values_hbm, precision_hbm, block_hbm, count_hbm, background_hbm,
    transition_hbm, start_hbm, filtered_ref, smoothed_ref,
    weights_ref, values_ref, precision_ref, block_ref, count_ref, background_ref, start_ref,
    transition_ref, local_sem,
    part, inbox, tiles, scatter_send, scatter_recv, gather_send, gather_recv,
    turned, gain_col, add_col, ahead_row, ahead_col, state_row, state_col, smooth_row, smooth_col,
):
    me = lax.axis_index("tm")
    steps, rows, width = weights_ref.shape
    size = transition_ref.shape[0]
    groups = size // 8
    loads = []
    for i, (source, held) in enumerate((
        (count_hbm, count_ref), (precision_hbm, precision_ref), (values_hbm, values_ref),
        (block_hbm, block_ref), (weights_hbm, weights_ref), (background_hbm, background_ref),
        (start_hbm, start_ref), (transition_hbm, transition_ref),
    )):
        loads.append(pltpu.make_async_copy(source, held, local_sem.at[i]))
        loads[-1].start()
    barrier = pltpu.get_barrier_semaphore()

    def greet(k, carry):
        pl.semaphore_signal(
            barrier, inc=1, device_id={"tm": lax.rem(me + k, n)}, device_id_type=MESH
        )
        return carry

    lax.fori_loop(1, n, greet, 0)
    for load in loads[:5]:
        load.wait()

    group = 8
    depth = group * rows
    lane = lax.broadcasted_iota(jnp.int32, (group, depth), 1)
    line = lax.broadcasted_iota(jnp.int32, (group, depth), 0)
    diagonal = lane // rows == line
    row = lax.broadcasted_iota(jnp.int32, (steps, rows), 1)
    count = jnp.broadcast_to(count_ref[...].astype(jnp.float32), (rows, steps)).T
    live = row < count.astype(jnp.int32)
    dot = functools.partial(jnp.dot, preferred_element_type=jnp.float32)
    for chunk in range(steps // group):
        here = pl.ds(chunk * group, group)
        weighted = jnp.where(
            live[chunk * group : (chunk + 1) * group], precision_ref[here, :], 0.0
        )
        moment = weighted * values_ref[here, :]
        which = block_ref[here, :]

        def left(coefficient):
            lines = []
            for b in range(2):
                chosen = jnp.where(which == b, coefficient, 0.0)
                wide = jnp.concatenate([chosen] * group, axis=1)
                lines.append(jnp.where(diagonal, wide, 0.0))
            high, low = two_parts(jnp.concatenate(lines, axis=0))
            return jnp.concatenate([high, low], axis=0)

        w = weights_ref[here].reshape(depth, width)
        wf = w.astype(jnp.float32)
        square_high, square_low = two_parts(wf * wf)
        info = dot(left(moment), w)
        info = info[: 2 * group] + info[2 * group :]
        lp = left(weighted)
        prec = dot(lp, square_high)
        prec = prec[: 2 * group] + prec[2 * group :] + dot(lp[: 2 * group], square_low)
        for kind, block in ((0, info), (1, prec)):
            for b in range(2):
                for j in range(group // 2):
                    part[chunk * (group // 2) + j, kind * 4 + b * 2 : kind * 4 + b * 2 + 2, :] = block[
                        b * group + 2 * j : b * group + 2 * j + 2
                    ]

    pl.semaphore_wait(barrier, n - 1)
    scatters = []
    for k in range(1, n):
        peer = lax.rem(me + k, n)
        copy = pltpu.make_async_remote_copy(
            src_ref=part.at[peer], dst_ref=inbox.at[k], send_sem=scatter_send.at[k],
            recv_sem=scatter_recv.at[k], device_id={"tm": peer}, device_id_type=MESH,
        )
        copy.start()
        scatters.append(copy)

    for load in loads[5:]:
        load.wait()

    def to_col(matrix, x, finish):
        left = jnp.broadcast_to(x[:, :LANES], (8, LANES))
        right = jnp.broadcast_to(x[:, LANES:], (8, LANES))
        for g in range(groups):
            at = pl.ds(8 * g, 8)
            p = matrix[at, :LANES] * left + matrix[at, LANES:] * right
            finish(at, jnp.broadcast_to(jnp.sum(p, axis=1, keepdims=True), (8, LANES)))

    def to_row(matrix, x_of):
        lines = 4
        totals = [[None, None] for _ in range(lines)]
        for g in range(groups):
            at = pl.ds(8 * g, 8)
            x = x_of(at)
            for h in range(2):
                p = matrix[at, h * LANES : (h + 1) * LANES] * x
                held = totals[g % lines][h]
                totals[g % lines][h] = p if held is None else held + p
        out = []
        for h in range(2):
            s = (totals[0][h] + totals[1][h]) + (totals[2][h] + totals[3][h])
            out.append(jnp.sum(s, axis=0, keepdims=True))
        return jnp.concatenate(out, axis=1)

    for i in range(2):
        for j in range(2):
            turned[j * LANES : (j + 1) * LANES, i * LANES : (i + 1) * LANES] = transition_ref[
                i * LANES : (i + 1) * LANES, j * LANES : (j + 1) * LANES
            ].T

    def keep_first(at, z):
        ahead_col[0, at, :] = z

    to_col(transition_ref, start_ref[...], keep_first)

    total = part[me]
    for k in range(1, n):
        scatters[k - 1].wait_recv()
        total = total + inbox[k]
    background = jnp.concatenate(
        [jnp.broadcast_to(background_ref[:, b * LANES : (b + 1) * LANES], (2, LANES)) for b in range(2)],
        axis=0,
    )
    denominator = background + total[4:]
    tiles[me] = jnp.concatenate([background / denominator, total[:4] / denominator], axis=0)
    gathers = []
    for k in range(1, n):
        peer = lax.rem(me + k, n)
        copy = pltpu.make_async_remote_copy(
            src_ref=tiles.at[me], dst_ref=tiles.at[me], send_sem=gather_send.at[k],
            recv_sem=gather_recv.at[me], device_id={"tm": peer}, device_id_type=MESH,
        )
        copy.start()
        gathers.append(copy)
    def arrive(d):
        @pl.when(d != me)
        def _():
            pltpu.make_async_remote_copy(
                src_ref=tiles.at[me], dst_ref=tiles.at[d], send_sem=gather_send.at[0],
                recv_sem=gather_recv.at[d], device_id={"tm": d}, device_id_type=MESH,
            ).wait_recv()

    def spread(d):
        held = tiles[d].T
        for b in range(2):
            at = pl.ds(b * LANES, LANES)
            for kind, kept in ((0, gain_col), (1, add_col)):
                c = kind * 4 + b * 2
                kept[d, at, :] = jnp.broadcast_to(held[:, c : c + 1], (LANES, LANES))

    def odd(d, kind):
        return jnp.concatenate([tiles[d, kind * 4 + b * 2 + 1 : kind * 4 + b * 2 + 2, :] for b in range(2)], axis=1)

    def to_odd(d):
        z = to_row(turned, lambda at: state_col[d, at, :])
        x = odd(d, 0) * z + odd(d, 1)
        ahead_row[d] = z
        state_row[d] = x
        return x

    def forward(d, x):
        def finish(at, z):
            ahead_col[d, at, :] = z
            state_col[d, at, :] = gain_col[d, at, :] * z + add_col[d, at, :]

        arrive(d + 1)
        to_col(transition_ref, x, finish)
        spread(d + 1)
        return to_odd(d)

    arrive(0)
    spread(0)
    state_col[0] = gain_col[0] * ahead_col[0] + add_col[0]
    arrive(1)
    spread(1)
    before = lax.fori_loop(1, n - 1, forward, to_odd(0))

    def finish_last(at, z):
        ahead_col[n - 1, at, :] = z
        state_col[n - 1, at, :] = gain_col[n - 1, at, :] * z + add_col[n - 1, at, :]

    to_col(transition_ref, before, finish_last)
    last = to_odd(n - 1)
    for copy in scatters:
        copy.wait_send()
    for copy in gathers:
        copy.wait_send()

    def to_even(d, s):
        def finish(at, y):
            smooth_col[d, at, :] = state_col[d, at, :] + gain_col[d, at, :] * y

        to_col(turned, s - ahead_row[d], finish)

    def backward(i, s):
        d = n - 1 - i
        to_even(d, s)
        y = to_row(transition_ref, lambda at: smooth_col[d, at, :] - ahead_col[d, at, :])
        s = state_row[d - 1] + odd(d - 1, 0) * y
        smooth_row[d - 1] = s
        return s

    smooth_row[n - 1] = last
    first = lax.fori_loop(0, n - 1, backward, last)
    to_even(0, first)

    corner = lax.broadcasted_iota(jnp.int32, (LANES, LANES), 0) == lax.broadcasted_iota(
        jnp.int32, (LANES, LANES), 1
    )
    for col, held, out in ((state_col, state_row, filtered_ref), (smooth_col, smooth_row, smoothed_ref)):
        for b in range(2):
            block = col[me, b * LANES : (b + 1) * LANES, :]
            out[0:1, b * LANES : (b + 1) * LANES] = jnp.sum(
                jnp.where(corner, block, 0.0), axis=0, keepdims=True
            )
        out[1:2, :] = held[me]


def hand_over(filtered_in, smoothed_in, filtered_ref, smoothed_ref, sem):
    first = pltpu.make_async_copy(filtered_in, filtered_ref, sem.at[0])
    second = pltpu.make_async_copy(smoothed_in, smoothed_ref, sem.at[1])
    first.start()
    second.start()
    first.wait()
    second.wait()


def shards(
    obs_weights, obs_values, obs_precision, obs_block, obs_count,
    prior_precision_entries, transition, initial_state,
):
    n = lax.axis_size("tm")
    size = transition.shape[0]
    row = pltpu.VMEM((n, 1, size), jnp.float32)
    col = pltpu.VMEM((n, size, LANES), jnp.float32)
    tile = pltpu.VMEM((n, 8, LANES), jnp.float32)
    out = jax.ShapeDtypeStruct((2, size), jnp.float32)
    inputs = (
        obs_weights, obs_values, obs_precision, obs_block, obs_count.T,
        prior_precision_entries[None], transition, initial_state[None],
    )
    order = (0, 1, 2, 3, 4, 5, 7, 6)
    results = pl.pallas_call(
        functools.partial(kernel, n),
        out_shape=(out, out),
        in_specs=[pl.BlockSpec(memory_space=pl.ANY)] * len(inputs),
        out_specs=(pl.BlockSpec(memory_space=pltpu.VMEM),) * 2,
        scratch_shapes=[pltpu.VMEM(inputs[i].shape, inputs[i].dtype) for i in order]
        + [pltpu.SemaphoreType.DMA((len(inputs),)), tile, tile, tile]
        + [pltpu.SemaphoreType.DMA((n,))] * 4
        + [pltpu.VMEM((size, size), jnp.float32), col, col, row, col, row, col, row, col],
        compiler_params=pltpu.CompilerParams(
            collective_id=0, has_side_effects=True, vmem_limit_bytes=60 * 1024 * 1024
        ),
        name="smoother",
    )(*inputs)
    return pl.pallas_call(
        hand_over,
        out_shape=(out, out),
        in_specs=[pl.BlockSpec(memory_space=pl.ANY)] * 2,
        out_specs=(pl.BlockSpec(memory_space=pl.ANY),) * 2,
        scratch_shapes=[pltpu.SemaphoreType.DMA((2,))],
        name="results",
    )(*results)


def solution(mesh):
    placed = (
        P("groups", "tm", None),
        P("groups", "tm"),
        P("groups", "tm"),
        P("groups", "tm"),
        P("groups", "tm"),
        P(),
        P(),
        P("groups"),
    )
    return jax.shard_map(
        shards,
        mesh=mesh,
        in_specs=placed,
        out_specs=(P(("groups", "tm"), None), P(("groups", "tm"), None)),
        check_vma=False,
    )
```

```python
import functools

import jax
import jax.numpy as jnp
from jax import lax
from jax.experimental import pallas as pl
from jax.experimental.pallas import tpu as pltpu
from jax.sharding import PartitionSpec as P

MESH = pl.DeviceIdType.MESH
LANES = 128


def two_parts(x):
    high = x.astype(jnp.bfloat16)
    low = (x - high.astype(jnp.float32)).astype(jnp.bfloat16)
    return high, low


def kernel(
    n, weights_hbm, values_hbm, precision_hbm, block_hbm, count_hbm, background_hbm,
    transition_hbm, start_hbm, filtered_ref, smoothed_ref,
    weights_ref, values_ref, precision_ref, block_ref, count_ref, background_ref, start_ref,
    transition_ref, local_sem,
    part, inbox, tiles, scatter_send, scatter_recv, gather_send, gather_recv,
    turned, gain_col, add_col, ahead_row, ahead_col, state_row, state_col, smooth_row, smooth_col,
):
    me = lax.axis_index("tm")
    steps, rows, width = weights_ref.shape
    size = transition_ref.shape[0]
    groups = size // 8
    loads = []
    for i, (source, held) in enumerate((
        (count_hbm, count_ref), (precision_hbm, precision_ref), (values_hbm, values_ref),
        (block_hbm, block_ref), (weights_hbm, weights_ref), (background_hbm, background_ref),
        (start_hbm, start_ref), (transition_hbm, transition_ref),
    )):
        loads.append(pltpu.make_async_copy(source, held, local_sem.at[i]))
        loads[-1].start()
    barrier = pltpu.get_barrier_semaphore()

    half = n // 2
    first_owner = n // 4
    mine = me - first_owner
    owning = (me >= first_owner) & (me < first_owner + half)

    def greet(k, carry):
        peer = lax.rem(me + k, n)

        @pl.when(owning | ((peer >= first_owner) & (peer < first_owner + half)))
        def _():
            pl.semaphore_signal(barrier, inc=1, device_id={"tm": peer}, device_id_type=MESH)

        return carry

    lax.fori_loop(1, n, greet, 0)
    for load in loads[:5]:
        load.wait()

    group = 8
    depth = group * rows
    lane = lax.broadcasted_iota(jnp.int32, (group, depth), 1)
    line = lax.broadcasted_iota(jnp.int32, (group, depth), 0)
    diagonal = lane // rows == line
    row = lax.broadcasted_iota(jnp.int32, (steps, rows), 1)
    count = jnp.broadcast_to(count_ref[...].astype(jnp.float32), (rows, steps)).T
    live = row < count.astype(jnp.int32)
    dot = functools.partial(jnp.dot, preferred_element_type=jnp.float32)
    for chunk in range(steps // group):
        here = pl.ds(chunk * group, group)
        weighted = jnp.where(
            live[chunk * group : (chunk + 1) * group], precision_ref[here, :], 0.0
        )
        moment = weighted * values_ref[here, :]
        which = block_ref[here, :]

        def left(coefficient):
            lines = []
            for b in range(2):
                chosen = jnp.where(which == b, coefficient, 0.0)
                wide = jnp.concatenate([chosen] * group, axis=1)
                lines.append(jnp.where(diagonal, wide, 0.0))
            high, low = two_parts(jnp.concatenate(lines, axis=0))
            return jnp.concatenate([high, low], axis=0)

        w = weights_ref[here].reshape(depth, width)
        wf = w.astype(jnp.float32)
        square_high, square_low = two_parts(wf * wf)
        info = dot(left(moment), w)
        info = info[: 2 * group] + info[2 * group :]
        lp = left(weighted)
        prec = dot(lp, square_high)
        prec = prec[: 2 * group] + prec[2 * group :] + dot(lp[: 2 * group], square_low)
        for kind, block in ((0, info), (1, prec)):
            for b in range(2):
                for j in range(group // 2):
                    part[chunk * (group // 2) + j, kind * 4 + b * 2 : kind * 4 + b * 2 + 2, :] = block[
                        b * group + 2 * j : b * group + 2 * j + 2
                    ]

    @pl.when(owning)
    def _():
        pl.semaphore_wait(barrier, n - 1)

    @pl.when(jnp.logical_not(owning))
    def _():
        pl.semaphore_wait(barrier, half)

    def scatter(o):
        return pltpu.make_async_remote_copy(
            src_ref=part.at[pl.ds(2 * o, 2)], dst_ref=inbox.at[me], send_sem=scatter_send.at[o],
            recv_sem=scatter_recv.at[me], device_id={"tm": first_owner + o}, device_id_type=MESH,
        )

    def incoming(s):
        return pltpu.make_async_remote_copy(
            src_ref=part.at[pl.ds(0, 2)], dst_ref=inbox.at[s], send_sem=scatter_send.at[0],
            recv_sem=scatter_recv.at[s], device_id={"tm": s}, device_id_type=MESH,
        )

    for j in range(half):
        o = lax.rem(me + j, half)

        @pl.when(o != mine)
        def _():
            scatter(o).start()

    for load in loads[5:]:
        load.wait()

    def to_col(matrix, x, finish):
        left = jnp.broadcast_to(x[:, :LANES], (8, LANES))
        right = jnp.broadcast_to(x[:, LANES:], (8, LANES))
        for g in range(groups):
            at = pl.ds(8 * g, 8)
            p = matrix[at, :LANES] * left + matrix[at, LANES:] * right
            finish(at, jnp.broadcast_to(jnp.sum(p, axis=1, keepdims=True), (8, LANES)))

    def to_row(matrix, x_of):
        lines = 4
        totals = [[None, None] for _ in range(lines)]
        for g in range(groups):
            at = pl.ds(8 * g, 8)
            x = x_of(at)
            for h in range(2):
                p = matrix[at, h * LANES : (h + 1) * LANES] * x
                held = totals[g % lines][h]
                totals[g % lines][h] = p if held is None else held + p
        out = []
        for h in range(2):
            s = (totals[0][h] + totals[1][h]) + (totals[2][h] + totals[3][h])
            out.append(jnp.sum(s, axis=0, keepdims=True))
        return jnp.concatenate(out, axis=1)

    for i in range(2):
        for j in range(2):
            turned[j * LANES : (j + 1) * LANES, i * LANES : (i + 1) * LANES] = transition_ref[
                i * LANES : (i + 1) * LANES, j * LANES : (j + 1) * LANES
            ].T

    def keep_first(at, z):
        ahead_col[0, at, :] = z

    to_col(transition_ref, start_ref[...], keep_first)

    background = jnp.concatenate(
        [jnp.broadcast_to(background_ref[:, b * LANES : (b + 1) * LANES], (2, LANES)) for b in range(2)],
        axis=0,
    )

    def gather(k):
        at = pl.ds(2 * mine, 2)
        return pltpu.make_async_remote_copy(
            src_ref=tiles.at[at], dst_ref=tiles.at[at], send_sem=gather_send.at[k],
            recv_sem=gather_recv.at[mine], device_id={"tm": lax.rem(me + k, n)},
            device_id_type=MESH,
        )

    @pl.when(owning)
    def _():
        totals = [part[2 * mine], part[2 * mine + 1]]
        for k in range(1, n):
            s = lax.rem(me + k, n)
            incoming(s).wait_recv()
            for t in range(2):
                totals[t] = totals[t] + inbox[s, t]
        for t in range(2):
            denominator = background + totals[t][4:]
            tiles[2 * mine + t] = jnp.concatenate(
                [background / denominator, totals[t][:4] / denominator], axis=0
            )
        for k in range(1, n):
            gather(k).start()

    def arrive(d):
        o = d // 2

        @pl.when((d % 2 == 0) & (o != mine))
        def _():
            at = pl.ds(2 * o, 2)
            pltpu.make_async_remote_copy(
                src_ref=tiles.at[at], dst_ref=tiles.at[at], send_sem=gather_send.at[0],
                recv_sem=gather_recv.at[o], device_id={"tm": first_owner + o},
                device_id_type=MESH,
            ).wait_recv()

    def spread(d):
        held = tiles[d].T
        for b in range(2):
            at = pl.ds(b * LANES, LANES)
            for kind, kept in ((0, gain_col), (1, add_col)):
                c = kind * 4 + b * 2
                kept[d, at, :] = jnp.broadcast_to(held[:, c : c + 1], (LANES, LANES))

    def odd(d, kind):
        return jnp.concatenate([tiles[d, kind * 4 + b * 2 + 1 : kind * 4 + b * 2 + 2, :] for b in range(2)], axis=1)

    def to_odd(d):
        z = to_row(turned, lambda at: state_col[d, at, :])
        x = odd(d, 0) * z + odd(d, 1)
        ahead_row[d] = z
        state_row[d] = x
        return x

    def forward(d, x):
        def finish(at, z):
            ahead_col[d, at, :] = z
            state_col[d, at, :] = gain_col[d, at, :] * z + add_col[d, at, :]

        arrive(d + 1)
        to_col(transition_ref, x, finish)
        spread(d + 1)
        return to_odd(d)

    arrive(0)
    spread(0)
    state_col[0] = gain_col[0] * ahead_col[0] + add_col[0]
    arrive(1)
    spread(1)
    before = lax.fori_loop(1, n - 1, forward, to_odd(0))

    def finish_last(at, z):
        ahead_col[n - 1, at, :] = z
        state_col[n - 1, at, :] = gain_col[n - 1, at, :] * z + add_col[n - 1, at, :]

    to_col(transition_ref, before, finish_last)
    last = to_odd(n - 1)
    for o in range(half):
        @pl.when(o != mine)
        def _():
            scatter(o).wait_send()

    @pl.when(owning)
    def _():
        for k in range(1, n):
            gather(k).wait_send()

    def to_even(d, s):
        def finish(at, y):
            smooth_col[d, at, :] = state_col[d, at, :] + gain_col[d, at, :] * y

        to_col(turned, s - ahead_row[d], finish)

    def backward(i, s):
        d = n - 1 - i
        to_even(d, s)
        y = to_row(transition_ref, lambda at: smooth_col[d, at, :] - ahead_col[d, at, :])
        s = state_row[d - 1] + odd(d - 1, 0) * y
        smooth_row[d - 1] = s
        return s

    smooth_row[n - 1] = last
    first = lax.fori_loop(0, n - 1, backward, last)
    to_even(0, first)

    corner = lax.broadcasted_iota(jnp.int32, (LANES, LANES), 0) == lax.broadcasted_iota(
        jnp.int32, (LANES, LANES), 1
    )
    for col, held, out in ((state_col, state_row, filtered_ref), (smooth_col, smooth_row, smoothed_ref)):
        for b in range(2):
            block = col[me, b * LANES : (b + 1) * LANES, :]
            out[0:1, b * LANES : (b + 1) * LANES] = jnp.sum(
                jnp.where(corner, block, 0.0), axis=0, keepdims=True
            )
        out[1:2, :] = held[me]


def hand_over(filtered_in, smoothed_in, filtered_ref, smoothed_ref, sem):
    first = pltpu.make_async_copy(filtered_in, filtered_ref, sem.at[0])
    second = pltpu.make_async_copy(smoothed_in, smoothed_ref, sem.at[1])
    first.start()
    second.start()
    first.wait()
    second.wait()


def shards(
    obs_weights, obs_values, obs_precision, obs_block, obs_count,
    prior_precision_entries, transition, initial_state,
):
    n = lax.axis_size("tm")
    size = transition.shape[0]
    row = pltpu.VMEM((n, 1, size), jnp.float32)
    col = pltpu.VMEM((n, size, LANES), jnp.float32)
    tile = pltpu.VMEM((n, 8, LANES), jnp.float32)
    inbox = pltpu.VMEM((n, 2, 8, LANES), jnp.float32)
    out = jax.ShapeDtypeStruct((2, size), jnp.float32)
    inputs = (
        obs_weights, obs_values, obs_precision, obs_block, obs_count.T,
        prior_precision_entries[None], transition, initial_state[None],
    )
    order = (0, 1, 2, 3, 4, 5, 7, 6)
    results = pl.pallas_call(
        functools.partial(kernel, n),
        out_shape=(out, out),
        in_specs=[pl.BlockSpec(memory_space=pl.ANY)] * len(inputs),
        out_specs=(pl.BlockSpec(memory_space=pltpu.VMEM),) * 2,
        scratch_shapes=[pltpu.VMEM(inputs[i].shape, inputs[i].dtype) for i in order]
        + [pltpu.SemaphoreType.DMA((len(inputs),)), tile, inbox, tile]
        + [pltpu.SemaphoreType.DMA((n,))] * 4
        + [pltpu.VMEM((size, size), jnp.float32), col, col, row, col, row, col, row, col],
        compiler_params=pltpu.CompilerParams(
            collective_id=0, has_side_effects=True, vmem_limit_bytes=60 * 1024 * 1024
        ),
        name="smoother",
    )(*inputs)
    return pl.pallas_call(
        hand_over,
        out_shape=(out, out),
        in_specs=[pl.BlockSpec(memory_space=pl.ANY)] * 2,
        out_specs=(pl.BlockSpec(memory_space=pl.ANY),) * 2,
        scratch_shapes=[pltpu.SemaphoreType.DMA((2,))],
        name="results",
    )(*results)


def solution(mesh):
    placed = (
        P("groups", "tm", None),
        P("groups", "tm"),
        P("groups", "tm"),
        P("groups", "tm"),
        P("groups", "tm"),
        P(),
        P(),
        P("groups"),
    )
    return jax.shard_map(
        shards,
        mesh=mesh,
        in_specs=placed,
        out_specs=(P(("groups", "tm"), None), P(("groups", "tm"), None)),
        check_vma=False,
    )
```
